256 devices in a mesh: modes: 64 (over z_hi, x, y, core), pix: 4 (over z_lo).
Axes of the slice: x: 4, y: 4, z: 8 (z_hi: 2, z_lo: 4; z = z_hi * 4 + z_lo), core: 2. Of those that a mesh axis runs over, the one named last changes fastest.
Arguments:
- pixel_modes: bfloat16 [2048, 98304], P('pix', 'modes'), may hold values from -6 to 6
- weighted_modes: bfloat16 [2048, 98304], P('pix', 'modes'), may hold values from -0.01171875 to 0.01171875
- mode_bins: int32 [98304], replicated, may hold values from 0 to 127
- live_counts: int32 [8, 2], P('pix'), may hold values from 17 to 128
Outputs:
- fisher_tiles: float32 [64, 5, 128, 128], P('modes')
The draws below stay inside these ranges and needn't reach their ends.
All inputs are finite; a program needn't handle non-finite values.
Results may differ from the reference program's by a relative error of at most 0.0003.
Values may be sent and summed in bfloat16 or wider, within the bound.
No kernel may reach another device: no remote copies, remote signals or barrier semaphores. Data moves between devices by JAX's collectives and lax.ppermute only.
A program may use at most 128 MiB of HBM per device.

```python
import jax
import jax.numpy as jnp
from jax import lax

MODES_DEV = 1536
NB = 128
SHELLS = 8
ROW_BLOCK = 128
ROUNDS = 5
PIXELS = 2048
BLOCKS = 2
MODES = 98304
N_MODES = 64


def draw_live_counts(key, part):
    key = jax.random.fold_in(key, 5)
    first, second, third = jax.random.split(key, 3)
    lowest = ROW_BLOCK // 8 + 1
    cells = SHELLS * BLOCKS
    values = jax.random.randint(first, (cells,), lowest, ROW_BLOCK + 1)
    top_spot = jax.random.randint(second, (), 0, cells)
    low_spot = jnp.mod(top_spot + 1 + jax.random.randint(third, (), 0, cells - 1), cells)
    places = jnp.arange(cells)
    values = jnp.where(places == top_spot, ROW_BLOCK, values)
    values = jnp.where(places == low_spot, lowest, values)
    return values.reshape(SHELLS, BLOCKS).astype(jnp.int32)


def set_ends(array, key, low, largest):
    shape = array.shape
    spot = [jax.random.randint(jax.random.fold_in(key, axis), (), 0, shape[axis]) for axis in range(len(shape))]
    array = array.at[tuple(spot)].set(low)
    longest = shape.index(max(shape))
    spot[longest] = (spot[longest] + 1) % shape[longest]
    return array.at[tuple(spot)].set(largest)


def levels(rng, dims, shards, low, largest):
    factor_of = 1.0
    for dim, blocks in shards:
        draws = jax.random.uniform(jax.random.fold_in(jax.random.fold_in(rng, 6), dim), (blocks,), jnp.float32, low / len(shards), largest / len(shards))
        factor_of = factor_of * jnp.repeat(jnp.exp(draws), dims[dim] // blocks).reshape((-1,) + (1,) * (len(dims) - 1 - dim))
    return factor_of


def scatter_about(own_key, shape, deviation, most, pieces=(), held_as=jnp.bfloat16):
    result = deviation * jax.random.normal(own_key, shape, jnp.float32)
    if pieces:
        result = result * levels(own_key, shape, pieces, -0.22, 0.18)
    return jnp.clip(result, -most, most).astype(held_as)


def setup_inputs(seed: int = 0) -> dict:
    key_of = jax.random.split(jax.random.key(seed), 5)
    pixel_modes = scatter_about(key_of[0], (PIXELS, MODES), 1.0, 6.0, ((0, 4), (1, 64)))
    weighted_modes = scatter_about(key_of[1], (PIXELS, MODES), (PIXELS * MODES_DEV * MODES_DEV // (NB * NB)) ** -0.5, 0.01171875, ((0, 4), (1, 64)))
    mode_bins = set_ends(jax.random.randint(key_of[2], (MODES,), 0, NB), jax.random.fold_in(key_of[2], 1), 0, NB - 1).astype(jnp.int32)
    live_counts = draw_live_counts(jax.random.fold_in(key_of[4], 71), 0)
    return {"pixel_modes": pixel_modes, "weighted_modes": weighted_modes, "mode_bins": mode_bins, "live_counts": live_counts}


def bin_table(bin_ids):
    return (bin_ids[:, None] == jnp.arange(NB, dtype=jnp.int32)[None, :]).astype(jnp.float32)


def reference(pixel_modes, weighted_modes, mode_bins, live_counts):
    offsets = jnp.arange(ROW_BLOCK, dtype=jnp.int32)
    live_rows = (offsets[None, None, :] < live_counts[:, :, None]).reshape(PIXELS)
    masked = pixel_modes * live_rows[:, None].astype(jnp.bfloat16)

    def one_block(block_index):
        own_cols = lax.dynamic_slice_in_dim(masked, block_index * MODES_DEV, MODES_DEV, 1)
        own_bins = lax.dynamic_slice_in_dim(mode_bins, block_index * MODES_DEV, MODES_DEV, 0)
        own_table = bin_table(own_bins)
        results = []
        for turn_index in range(ROUNDS):
            partner = jnp.mod(block_index - turn_index - 1, N_MODES).astype(jnp.int32)
            other_cols = lax.dynamic_slice_in_dim(weighted_modes, partner * MODES_DEV, MODES_DEV, 1)
            other_bins = lax.dynamic_slice_in_dim(mode_bins, partner * MODES_DEV, MODES_DEV, 0)
            tile = jnp.dot(own_cols.T, other_cols, preferred_element_type=jnp.float32)
            squares = tile * tile
            left = jnp.dot(own_table.T, squares, precision=lax.Precision.HIGHEST)
            results.append(0.5 * jnp.dot(left, bin_table(other_bins), precision=lax.Precision.HIGHEST))
        return jnp.stack(results)

    return lax.map(one_block, jnp.arange(N_MODES, dtype=jnp.int32))
```

```python
import jax
import jax.numpy as jnp
from jax import lax
from jax.sharding import PartitionSpec as P

NB = 128
ROW_BLOCK = 128
ROUNDS = 5
CHUNKS = 3
GROUPS = 4
HALF = 32


def move(block, route):
    pairs = []
    for half in range(2):
        for place in range(HALF):
            for p in range(GROUPS):
                target = route(half, place, p)
                if target is not None:
                    source = (half * HALF + place) * GROUPS + p
                    pairs.append((source, (target[0] * HALF + target[1]) * GROUPS + target[2]))
    return lax.ppermute(block, ("modes", "pix"), pairs)


def ahead(distance, core=None, wrap=False):
    def route(half, place, p):
        if core is not None and place % 2 != core:
            return None
        if (place + distance >= HALF) != wrap:
            return None
        return half, (place + distance) % HALF, p

    return route


def across(half, place, p):
    if place < HALF - ROUNDS:
        return None
    return 1 - half, place, GROUPS - 1 - p


def other_core(half, place, p):
    return half, place ^ 1, p


def core_up(half, place, p):
    return (half, place + 1, p) if place % 2 == 0 else None


def pix_partner(k):
    return lambda half, place, p: (half, place, p ^ k)


def bin_table(bin_ids):
    return (bin_ids[:, None] == jnp.arange(NB, dtype=jnp.int32)[None, :]).astype(jnp.float32)


def bin_tile(flipped, partner_bins, own_table):
    squares = flipped * flipped
    partner_table = bin_table(partner_bins)
    left = lax.dot_general(
        partner_table, squares, (((0,), (0,)), ((), ())), precision=lax.Precision.HIGHEST
    )
    return 0.5 * jnp.dot(left, own_table, precision=lax.Precision.HIGHEST).T


def sum_over_pix(part, pix_index):
    rows = NB // GROUPS

    def piece(k):
        return lax.dynamic_slice_in_dim(part, (pix_index ^ k) * rows, rows, 1)

    total = piece(0)
    for k in range(1, GROUPS):
        total = total + move(piece(k), pix_partner(k))
    out = jnp.zeros_like(part)
    for k in range(GROUPS):
        got = total if k == 0 else move(total, pix_partner(k))
        out = lax.dynamic_update_slice_in_dim(out, got, (pix_index ^ k) * rows, 1)
    return out


def shards(pixel_modes, weighted_modes, mode_bins, live_counts):
    row_count, col_count = pixel_modes.shape
    cycle_size = lax.axis_size("modes")
    quarter = col_count // GROUPS
    own_index = lax.axis_index("modes")
    pix_index = lax.axis_index("pix")
    core = own_index % 2
    place = own_index % HALF
    offsets = lax.broadcasted_iota(
        jnp.int32, (live_counts.shape[0], live_counts.shape[1], ROW_BLOCK), 2
    )
    live_rows = (offsets < live_counts[:, :, None]).reshape(row_count)

    carried = lax.all_to_all(weighted_modes, "pix", split_axis=1, concat_axis=0, tiled=True)
    shadow = move(carried, across)
    near = move(carried, ahead(2))
    far = move(carried, ahead(4))
    last = move(carried, ahead(5, core=1))

    masked = pixel_modes * live_rows[:, None].astype(jnp.bfloat16)
    width = col_count // CHUNKS
    full = []
    gate = carried
    for c in range(CHUNKS):
        chunk = masked[:, c * width : (c + 1) * width]
        chunk, _ = lax.optimization_barrier((chunk, gate))
        full.append(lax.all_gather(chunk, "pix", axis=0, tiled=True))
        gate = full[-1]

    near = jnp.where(place < 2, move(shadow, ahead(2, wrap=True)), near)
    far = jnp.where(place < 4, move(shadow, ahead(4, wrap=True)), far)
    last = jnp.where(place < 5, move(shadow, ahead(5, core=1, wrap=True)), last)
    first = move(jnp.where(core == 0, carried, near), other_core)
    third = move(jnp.where(core == 0, near, far), other_core)
    fifth = jnp.where(core == 0, last, move(far, core_up))
    partners = [first, near, third, far, fifth]

    own_bins = lax.dynamic_slice_in_dim(mode_bins, own_index * col_count, col_count, 0)
    own_table = bin_table(own_bins)
    binned = []
    for turn_index in range(ROUNDS):
        owner_index = jnp.mod(own_index - turn_index - 1, cycle_size)
        same_half = owner_index // HALF == own_index // HALF
        which = jnp.where(same_half, pix_index, GROUPS - 1 - pix_index)
        partner_bins = lax.dynamic_slice_in_dim(
            mode_bins, owner_index * col_count + which * quarter, quarter, 0
        )
        total = 0.0
        for c in range(CHUNKS):
            flipped = lax.dot_general(
                partners[turn_index], full[c], (((0,), (0,)), ((), ())),
                preferred_element_type=jnp.float32,
            )
            total = total + bin_tile(flipped, partner_bins, own_table[c * width : (c + 1) * width])
        binned.append(total)
    return sum_over_pix(jnp.stack(binned), pix_index)[None]


def solution(mesh):
    in_specs = (P("pix", "modes"), P("pix", "modes"), P(), P("pix", None))
    out_specs = P("modes", None, None, None)
    return jax.shard_map(shards, mesh=mesh, in_specs=in_specs, out_specs=out_specs, check_vma=False)
```

```python
import jax
import jax.numpy as jnp
from jax import lax
from jax.sharding import PartitionSpec as P

NB = 128
ROW_BLOCK = 128
ROUNDS = 5
GROUPS = 4
HALF = 32


def move(block, route):
    pairs = []
    for half in range(2):
        for place in range(HALF):
            for p in range(GROUPS):
                target = route(half, place, p)
                if target is not None:
                    source = (half * HALF + place) * GROUPS + p
                    pairs.append((source, (target[0] * HALF + target[1]) * GROUPS + target[2]))
    return lax.ppermute(block, ("modes", "pix"), pairs)


def spot(place):
    return place // 8, (place // 2) % 4, place % 2


def seat(x, y, core):
    return (x * 4 + y) * 2 + core


def trails(y, core):
    return 2 * y + core >= 8 - ROUNDS


def next_row(half, place, p):
    x, y, core = spot(place)
    return (half, seat(x + 1, y, core), p) if x < 3 and trails(y, core) else None


def next_half(k):
    def route(half, place, p):
        x, y, core = spot(place)
        return (1 - half, seat(0, y, core), (GROUPS - 1 - p) ^ k) if x == 3 and trails(y, core) else None

    return route


def along_row(chips, wrap, last=False):
    def route(half, place, p):
        x, y, core = spot(place)
        if (y + chips >= 4) != wrap or (last and core == 0):
            return None
        return half, seat(x, (y + chips) % 4, 0 if last else core), p

    return route


def other_core(half, place, p):
    return half, place ^ 1, p


def core_up(half, place, p):
    return (half, place + 1, p) if place % 2 == 0 else None


def pix_partner(k):
    return lambda half, place, p: (half, place, p ^ k)


def bin_table(bin_ids):
    return (bin_ids[:, None] == jnp.arange(NB, dtype=jnp.int32)[None, :]).astype(jnp.float32)


def bin_tile(flipped, partner_bins, own_table):
    squares = flipped * flipped
    partner_table = bin_table(partner_bins)
    left = lax.dot_general(
        partner_table, squares, (((0,), (0,)), ((), ())), precision=lax.Precision.HIGHEST
    )
    return 0.5 * jnp.dot(left, own_table, precision=lax.Precision.HIGHEST).T


def sum_over_pix(part, pix_index):
    rows = NB // GROUPS

    def piece(k):
        return lax.dynamic_slice_in_dim(part, (pix_index ^ k) * rows, rows, 1)

    total = piece(0)
    for k in range(1, GROUPS):
        total = total + move(piece(k), pix_partner(k))
    out = jnp.zeros_like(part)
    for k in range(GROUPS):
        got = total if k == 0 else move(total, pix_partner(k))
        out = lax.dynamic_update_slice_in_dim(out, got, (pix_index ^ k) * rows, 1)
    return out


def shards(pixel_modes, weighted_modes, mode_bins, live_counts):
    row_count, col_count = pixel_modes.shape
    cycle_size = lax.axis_size("modes")
    quarter = col_count // GROUPS
    own_index = lax.axis_index("modes")
    pix_index = lax.axis_index("pix")
    x, y, core = spot(own_index % HALF)
    offsets = lax.broadcasted_iota(
        jnp.int32, (live_counts.shape[0], live_counts.shape[1], ROW_BLOCK), 2
    )
    live_rows = (offsets < live_counts[:, :, None]).reshape(row_count)

    masked = pixel_modes * live_rows[:, None].astype(jnp.bfloat16)
    full = lax.all_gather(masked, "pix", axis=0, tiled=True)
    carried = lax.all_to_all(weighted_modes, "pix", split_axis=1, concat_axis=0, tiled=True)

    crossed = jnp.zeros_like(carried)
    for k in range(GROUPS):
        target = (GROUPS - 1 - pix_index) ^ k
        piece = lax.dynamic_slice_in_dim(weighted_modes, target * quarter, quarter, 1)
        got = move(piece, next_half(k))
        source = (pix_index ^ k) ^ (GROUPS - 1)
        crossed = lax.dynamic_update_slice_in_dim(crossed, got, source * row_count, 0)
    previous = jnp.where(x == 0, crossed, move(carried, next_row))

    near = jnp.where(y < 1, move(previous, along_row(1, True)), move(carried, along_row(1, False)))
    far = jnp.where(y < 2, move(previous, along_row(2, True)), move(carried, along_row(2, False)))
    last = jnp.where(
        y < 3, move(previous, along_row(3, True, True)), move(carried, along_row(3, False, True))
    )
    first = move(jnp.where(core == 0, carried, near), other_core)
    third = move(jnp.where(core == 0, near, far), other_core)
    fifth = jnp.where(core == 0, last, move(far, core_up))
    partners = [first, near, third, far, fifth]

    own_bins = lax.dynamic_slice_in_dim(mode_bins, own_index * col_count, col_count, 0)
    own_table = bin_table(own_bins)
    binned = []
    for turn_index in range(ROUNDS):
        owner_index = jnp.mod(own_index - turn_index - 1, cycle_size)
        partner_bins = lax.dynamic_slice_in_dim(
            mode_bins, owner_index * col_count + pix_index * quarter, quarter, 0
        )
        flipped = lax.dot_general(
            partners[turn_index], full, (((0,), (0,)), ((), ())), preferred_element_type=jnp.float32
        )
        total = bin_tile(flipped, partner_bins, own_table)
        binned.append(total)
    return sum_over_pix(jnp.stack(binned), pix_index)[None]


def solution(mesh):
    in_specs = (P("pix", "modes"), P("pix", "modes"), P(), P("pix", None))
    out_specs = P("modes", None, None, None)
    return jax.shard_map(shards, mesh=mesh, in_specs=in_specs, out_specs=out_specs, check_vma=False)
```

```python
import functools

import jax
import jax.numpy as jnp
from jax import lax
from jax.sharding import PartitionSpec as P

NB = 128
ROW_BLOCK = 128
ROUNDS = 5
GROUPS = 4
HALF = 32
SIZES = (320, 384, 448, 512)


def move(block, route):
    pairs = []
    for half in range(2):
        for place in range(HALF):
            for p in range(GROUPS):
                target = route(half, place, p)
                if target is not None:
                    source = (half * HALF + place) * GROUPS + p
                    pairs.append((source, (target[0] * HALF + target[1]) * GROUPS + target[2]))
    return lax.ppermute(block, ("modes", "pix"), pairs)


def spot(place):
    return place // 8, (place // 2) % 4, place % 2


def seat(x, y, core):
    return (x * 4 + y) * 2 + core


def trails(y, core):
    return 2 * y + core >= 8 - ROUNDS


def next_row(half, place, p):
    x, y, core = spot(place)
    return (half, seat(x + 1, y, core), p) if x < 3 and trails(y, core) else None


def next_half(k):
    def route(half, place, p):
        x, y, core = spot(place)
        return (1 - half, seat(0, y, core), p ^ k) if x == 3 and trails(y, core) else None

    return route


def along_row(chips, wrap, last=False):
    def route(half, place, p):
        x, y, core = spot(place)
        if (y + chips >= 4) != wrap or (last and core == 0):
            return None
        return half, seat(x, (y + chips) % 4, 0 if last else core), p

    return route


def other_core(half, place, p):
    return half, place ^ 1, p


def core_up(half, place, p):
    return (half, place + 1, p) if place % 2 == 0 else None


def pix_partner(k):
    return lambda half, place, p: (half, place, p ^ k)


def bin_table(bin_ids):
    return (bin_ids[:, None] == jnp.arange(NB, dtype=jnp.int32)[None, :]).astype(jnp.float32)


def bin_tile(flipped, partner_bins, own_table):
    squares = flipped * flipped
    partner_table = bin_table(partner_bins)
    left = lax.dot_general(
        partner_table, squares, (((0,), (0,)), ((), ())), precision=lax.Precision.HIGHEST
    )
    return 0.5 * jnp.dot(left, own_table, precision=lax.Precision.HIGHEST).T


def sum_over_pix(part, pix_index):
    rows = NB // GROUPS

    def piece(k):
        return lax.dynamic_slice_in_dim(part, (pix_index ^ k) * rows, rows, 1)

    total = piece(0)
    for k in range(1, GROUPS):
        total = total + move(piece(k), pix_partner(k))
    out = jnp.zeros_like(part)
    for k in range(GROUPS):
        got = total if k == 0 else move(total, pix_partner(k))
        out = lax.dynamic_update_slice_in_dim(out, got, (pix_index ^ k) * rows, 1)
    return out


def packing(live_counts):
    counts = live_counts.reshape(-1)
    ends = jnp.cumsum(counts)
    offsets = jnp.arange(ROW_BLOCK, dtype=jnp.int32)[None, :]
    places = jnp.where(offsets < counts[:, None], (ends - counts)[:, None] + offsets, -1).reshape(-1)
    return (jnp.arange(places.shape[0], dtype=jnp.int32)[:, None] == places[None, :]).astype(jnp.bfloat16)


def largest_over_pix(count):
    held = jnp.full((8, 128), count, jnp.float32)
    most = held
    for k in range(1, GROUPS):
        most = jnp.maximum(most, move(held, pix_partner(k)))
    return most[0, 0].astype(jnp.int32)


def tiles(row_count, masked, weighted, mode_bins):
    masked, weighted = masked[:row_count], weighted[:row_count]
    col_count = masked.shape[1]
    cycle_size = lax.axis_size("modes")
    quarter = col_count // GROUPS
    own_index = lax.axis_index("modes")
    pix_index = lax.axis_index("pix")
    x, y, core = spot(own_index % HALF)

    full = lax.all_gather(masked, "pix", axis=0, tiled=True)

    pieces = [
        lax.dynamic_slice_in_dim(weighted, (pix_index ^ k) * quarter, quarter, 1)
        for k in range(GROUPS)
    ]

    def in_order(got):
        out = jnp.zeros((GROUPS * row_count, quarter), jnp.bfloat16)
        for k in range(GROUPS):
            out = lax.dynamic_update_slice_in_dim(out, got[k], (pix_index ^ k) * row_count, 0)
        return out

    crossed = in_order([move(pieces[k], next_half(k)) for k in range(GROUPS)])
    carried = in_order([pieces[0]] + [move(pieces[k], pix_partner(k)) for k in range(1, GROUPS)])
    previous = jnp.where(x == 0, crossed, move(carried, next_row))

    near = jnp.where(y < 1, move(previous, along_row(1, True)), move(carried, along_row(1, False)))
    far = jnp.where(y < 2, move(previous, along_row(2, True)), move(carried, along_row(2, False)))
    last = jnp.where(
        y < 3, move(previous, along_row(3, True, True)), move(carried, along_row(3, False, True))
    )
    first = move(jnp.where(core == 0, carried, near), other_core)
    third = move(jnp.where(core == 0, near, far), other_core)
    fifth = jnp.where(core == 0, last, move(far, core_up))
    partners = [first, near, third, far, fifth]

    own_bins = lax.dynamic_slice_in_dim(mode_bins, own_index * col_count, col_count, 0)
    own_table = bin_table(own_bins)
    binned = []
    for turn_index in range(ROUNDS):
        owner_index = jnp.mod(own_index - turn_index - 1, cycle_size)
        partner_bins = lax.dynamic_slice_in_dim(
            mode_bins, owner_index * col_count + pix_index * quarter, quarter, 0
        )
        flipped = lax.dot_general(
            partners[turn_index], full, (((0,), (0,)), ((), ())), preferred_element_type=jnp.float32
        )
        binned.append(bin_tile(flipped, partner_bins, own_table))
    return sum_over_pix(jnp.stack(binned), pix_index)[None]


def shards(pixel_modes, weighted_modes, mode_bins, live_counts):
    most = largest_over_pix(jnp.sum(live_counts))
    pack = packing(live_counts)
    masked = jnp.dot(pack, pixel_modes)
    weighted = jnp.dot(pack, weighted_modes)
    level = sum((most > size).astype(jnp.int32) for size in SIZES[:-1])
    return lax.switch(level, [functools.partial(tiles, size) for size in SIZES], masked, weighted, mode_bins)


def solution(mesh):
    in_specs = (P("pix", "modes"), P("pix", "modes"), P(), P("pix", None))
    out_specs = P("modes", None, None, None)
    return jax.shard_map(shards, mesh=mesh, in_specs=in_specs, out_specs=out_specs, check_vma=False)
```

```python
import functools

import jax
import jax.numpy as jnp
from jax import lax
from jax.sharding import PartitionSpec as P

NB = 128
ROW_BLOCK = 128
ROUNDS = 5
GROUPS = 4
HALF = 32
SIZES = (320, 384, 448, 512)


def move(block, route):
    pairs = []
    for half in range(2):
        for place in range(HALF):
            for p in range(GROUPS):
                target = route(half, place, p)
                if target is not None:
                    source = (half * HALF + place) * GROUPS + p
                    pairs.append((source, (target[0] * HALF + target[1]) * GROUPS + target[2]))
    return lax.ppermute(block, ("modes", "pix"), pairs)


def spot(place):
    return place // 8, (place // 2) % 4, place % 2


def seat(x, y, core):
    return (x * 4 + y) * 2 + core


def trails(y, core):
    return 2 * y + core >= 8 - ROUNDS


def next_row(half, place, p):
    x, y, core = spot(place)
    return (half, seat(x + 1, y, core), p) if x < 3 and trails(y, core) else None


def across(k, column):
    def route(half, place, p):
        x, y, core = spot(place)
        return (1 - half, place, p ^ k) if x == column and trails(y, core) else None

    return route


def around(half, place, p):
    x, y, core = spot(place)
    return (half, seat(0, y, core), p) if x == 3 and trails(y, core) else None


def along_row(chips, wrap, last=False):
    def route(half, place, p):
        x, y, core = spot(place)
        if (y + chips >= 4) != wrap or (last and core == 0):
            return None
        return half, seat(x, (y + chips) % 4, 0 if last else core), p

    return route


def other_core(half, place, p):
    return half, place ^ 1, p


def core_up(half, place, p):
    return (half, place + 1, p) if place % 2 == 0 else None


def pix_partner(k):
    return lambda half, place, p: (half, place, p ^ k)


def bin_table(bin_ids):
    return (bin_ids[:, None] == jnp.arange(NB, dtype=jnp.int32)[None, :]).astype(jnp.float32)


def bin_tile(flipped, partner_bins, own_table):
    squares = flipped * flipped
    partner_table = bin_table(partner_bins)
    left = lax.dot_general(
        partner_table, squares, (((0,), (0,)), ((), ())), precision=lax.Precision.HIGHEST
    )
    return 0.5 * jnp.dot(left, own_table, precision=lax.Precision.HIGHEST).T


def sum_over_pix(part, pix_index):
    rows = NB // GROUPS

    def piece(k):
        return lax.dynamic_slice_in_dim(part, (pix_index ^ k) * rows, rows, 1)

    total = piece(0)
    for k in range(1, GROUPS):
        total = total + move(piece(k), pix_partner(k))
    out = jnp.zeros_like(part)
    for k in range(GROUPS):
        got = total if k == 0 else move(total, pix_partner(k))
        out = lax.dynamic_update_slice_in_dim(out, got, (pix_index ^ k) * rows, 1)
    return out


def packing(live_counts):
    counts = live_counts.reshape(-1)
    ends = jnp.cumsum(counts)
    offsets = jnp.arange(ROW_BLOCK, dtype=jnp.int32)[None, :]
    places = jnp.where(offsets < counts[:, None], (ends - counts)[:, None] + offsets, -1).reshape(-1)
    return (jnp.arange(places.shape[0], dtype=jnp.int32)[:, None] == places[None, :]).astype(jnp.bfloat16)


def largest_over_pix(count):
    held = jnp.full((8, 128), count, jnp.float32)
    most = held
    for k in range(1, GROUPS):
        most = jnp.maximum(most, move(held, pix_partner(k)))
    return most[0, 0].astype(jnp.int32)


def tiles(row_count, masked, weighted, mode_bins):
    masked, weighted = masked[:row_count], weighted[:row_count]
    col_count = masked.shape[1]
    cycle_size = lax.axis_size("modes")
    quarter = col_count // GROUPS
    own_index = lax.axis_index("modes")
    pix_index = lax.axis_index("pix")
    x, y, core = spot(own_index % HALF)

    pieces = [
        lax.dynamic_slice_in_dim(weighted, (pix_index ^ k) * quarter, quarter, 1)
        for k in range(GROUPS)
    ]

    def in_order(got):
        out = jnp.zeros((GROUPS * row_count, quarter), jnp.bfloat16)
        for k in range(GROUPS):
            out = lax.dynamic_update_slice_in_dim(out, got[k], (pix_index ^ k) * row_count, 0)
        return out

    swapped = [move(pieces[k], pix_partner(k)) for k in range(1, GROUPS)]
    early = [move(pieces[k], across(k, 3)) for k in (0, 3)]
    late = move(jnp.concatenate([pieces[1], pieces[2]]), around)
    masked, swapped, early, late = lax.optimization_barrier((masked, swapped, early, late))

    full = lax.all_gather(masked, "pix", axis=0, tiled=True)
    carried = in_order([pieces[0]] + swapped)
    early = move(jnp.concatenate(early), around)
    late = [move(late[:row_count], across(1, 0)), move(late[row_count:], across(2, 0))]
    crossed = in_order([early[:row_count]] + late + [early[row_count:]])
    previous = jnp.where(x == 0, crossed, move(carried, next_row))

    near = jnp.where(y < 1, move(previous, along_row(1, True)), move(carried, along_row(1, False)))
    far = jnp.where(y < 2, move(previous, along_row(2, True)), move(carried, along_row(2, False)))
    last = jnp.where(
        y < 3, move(previous, along_row(3, True, True)), move(carried, along_row(3, False, True))
    )
    first = move(jnp.where(core == 0, carried, near), other_core)
    third = move(jnp.where(core == 0, near, far), other_core)
    fifth = jnp.where(core == 0, last, move(far, core_up))
    partners = [first, near, third, far, fifth]

    own_bins = lax.dynamic_slice_in_dim(mode_bins, own_index * col_count, col_count, 0)
    own_table = bin_table(own_bins)
    binned = []
    for turn_index in range(ROUNDS):
        owner_index = jnp.mod(own_index - turn_index - 1, cycle_size)
        partner_bins = lax.dynamic_slice_in_dim(
            mode_bins, owner_index * col_count + pix_index * quarter, quarter, 0
        )
        flipped = lax.dot_general(
            partners[turn_index], full, (((0,), (0,)), ((), ())), preferred_element_type=jnp.float32
        )
        binned.append(bin_tile(flipped, partner_bins, own_table))
    return sum_over_pix(jnp.stack(binned), pix_index)[None]


def shards(pixel_modes, weighted_modes, mode_bins, live_counts):
    most = largest_over_pix(jnp.sum(live_counts))
    pack = packing(live_counts)
    masked = jnp.dot(pack, pixel_modes)
    weighted = jnp.dot(pack, weighted_modes)
    level = sum((most > size).astype(jnp.int32) for size in SIZES[:-1])
    return lax.switch(level, [functools.partial(tiles, size) for size in SIZES], masked, weighted, mode_bins)


def solution(mesh):
    in_specs = (P("pix", "modes"), P("pix", "modes"), P(), P("pix", None))
    out_specs = P("modes", None, None, None)
    return jax.shard_map(shards, mesh=mesh, in_specs=in_specs, out_specs=out_specs, check_vma=False)
```

```python
import functools

import jax
import jax.numpy as jnp
from jax import lax
from jax.experimental import pallas as pl
from jax.experimental.pallas import tpu as pltpu
from jax.sharding import PartitionSpec as P

NB = 128
ROW_BLOCK = 128
ROUNDS = 5
GROUPS = 4
HALF = 32
CHUNKS = 3
SIZES = (320, 384, 448, 512)


def move(block, route):
    pairs = []
    for half in range(2):
        for place in range(HALF):
            for p in range(GROUPS):
                target = route(half, place, p)
                if target is not None:
                    source = (half * HALF + place) * GROUPS + p
                    pairs.append((source, (target[0] * HALF + target[1]) * GROUPS + target[2]))
    return lax.ppermute(block, ("modes", "pix"), pairs)


def spot(place):
    return place // 8, (place // 2) % 4, place % 2


def seat(x, y, core):
    return (x * 4 + y) * 2 + core


def trails(y, core):
    return 2 * y + core >= 8 - ROUNDS


def next_row(half, place, p):
    x, y, core = spot(place)
    return (half, seat(x + 1, y, core), p) if x < 3 and trails(y, core) else None


def across(k, column):
    def route(half, place, p):
        x, y, core = spot(place)
        return (1 - half, place, p ^ k) if x == column and trails(y, core) else None

    return route


def around(half, place, p):
    x, y, core = spot(place)
    return (half, seat(0, y, core), p) if x == 3 and trails(y, core) else None


def along_row(chips, wrap, last=False):
    def route(half, place, p):
        x, y, core = spot(place)
        if (y + chips >= 4) != wrap or (last and core == 0):
            return None
        return half, seat(x, (y + chips) % 4, 0 if last else core), p

    return route


def other_core(half, place, p):
    return half, place ^ 1, p


def core_up(half, place, p):
    return (half, place + 1, p) if place % 2 == 0 else None


def pix_partner(k):
    return lambda half, place, p: (half, place, p ^ k)


def bin_kernel(own_ref, partner_ref, full_ref, *rest):
    partner_cols, (out_ref, full, partner, own_table, full_sems, partner_sems) = rest[:ROUNDS], rest[ROUNDS:]
    quarter = partner.shape[2]
    width = full.shape[1] // CHUNKS

    def full_copy(c):
        part = pl.ds(c * width, width)
        return pltpu.make_async_copy(full_ref.at[:, part], full.at[:, part], full_sems.at[c])

    def partner_copy(r):
        return pltpu.make_async_copy(partner_cols[r], partner.at[r], partner_sems.at[r])

    partner_copy(0).start()
    for c in range(CHUNKS):
        full_copy(c).start()
    for r in range(1, ROUNDS):
        partner_copy(r).start()
    bins = lax.broadcasted_iota(jnp.int32, (NB, 1), 0)
    own_table[...] = (bins == own_ref[...]).astype(jnp.bfloat16).T

    def parts(values):
        high = values.astype(jnp.bfloat16)
        return high, (values - high.astype(jnp.float32)).astype(jnp.bfloat16)

    def product(r, c):
        if c == 0:
            partner_copy(r).wait()
        if r == 0:
            full_copy(c).wait()
        return lax.dot_general(
            partner[r], full[:, c * width : (c + 1) * width], (((0,), (0,)), ((), ())),
            preferred_element_type=jnp.float32,
        )

    steps = [(r, c) for r in range(ROUNDS) for c in range(CHUNKS)]
    upcoming = product(0, 0)
    for step, (r, c) in enumerate(steps):
        tile = upcoming
        if step + 1 < len(steps):
            upcoming = product(*steps[step + 1])
        if c == 0:
            left = jnp.zeros((quarter, NB), jnp.float32)
        for part in parts(tile * tile):
            left = left + jnp.dot(
                part, own_table[c * width : (c + 1) * width, :], preferred_element_type=jnp.float32
            )
        if c == CHUNKS - 1:
            table = (bins == partner_ref[r : r + 1, :]).astype(jnp.bfloat16)
            total = jnp.zeros((NB, NB), jnp.float32)
            for part in parts(left):
                total = total + jnp.dot(table, part, preferred_element_type=jnp.float32)
            out_ref[r] = (0.5 * total).T


def bin_tiles(full, partners, own_bins, partner_bins):
    depth, col_count = full.shape
    quarter = partners[0].shape[1]
    whole = pl.BlockSpec(memory_space=pltpu.VMEM)
    anywhere = pl.BlockSpec(memory_space=pl.ANY)
    macs = ROUNDS * depth * col_count * quarter
    return pl.pallas_call(
        bin_kernel,
        out_shape=jax.ShapeDtypeStruct((ROUNDS, NB, NB), jnp.float32),
        in_specs=[whole, whole] + [anywhere] * (1 + ROUNDS),
        out_specs=whole,
        scratch_shapes=[
            pltpu.VMEM((depth, col_count), jnp.bfloat16),
            pltpu.VMEM((ROUNDS, depth, quarter), jnp.bfloat16),
            pltpu.VMEM((col_count, NB), jnp.bfloat16),
            pltpu.SemaphoreType.DMA((CHUNKS,)),
            pltpu.SemaphoreType.DMA((ROUNDS,)),
        ],
        compiler_params=pltpu.CompilerParams(vmem_limit_bytes=40 * 1024 * 1024),
        cost_estimate=pl.CostEstimate(
            flops=3 * macs, bytes_accessed=2 * depth * (col_count + ROUNDS * quarter), transcendentals=0
        ),
    )(own_bins[None, :], partner_bins, full, *partners)


def sum_over_pix(part, pix_index):
    rows = NB // GROUPS

    def piece(k):
        return lax.dynamic_slice_in_dim(part, (pix_index ^ k) * rows, rows, 1)

    total = piece(0)
    for k in range(1, GROUPS):
        total = total + move(piece(k), pix_partner(k))
    out = jnp.zeros_like(part)
    for k in range(GROUPS):
        got = total if k == 0 else move(total, pix_partner(k))
        out = lax.dynamic_update_slice_in_dim(out, got, (pix_index ^ k) * rows, 1)
    return out


def packing(live_counts):
    counts = live_counts.reshape(-1)
    ends = jnp.cumsum(counts)
    offsets = jnp.arange(ROW_BLOCK, dtype=jnp.int32)[None, :]
    places = jnp.where(offsets < counts[:, None], (ends - counts)[:, None] + offsets, -1).reshape(-1)
    return (jnp.arange(places.shape[0], dtype=jnp.int32)[:, None] == places[None, :]).astype(jnp.bfloat16)


def largest_over_pix(count):
    held = jnp.full((8, 128), count, jnp.float32)
    most = held
    for k in range(1, GROUPS):
        most = jnp.maximum(most, move(held, pix_partner(k)))
    return most[0, 0].astype(jnp.int32)


def tiles(row_count, pack, pixel_modes, weighted_modes, mode_bins):
    pack = pack[:row_count]
    col_count = pixel_modes.shape[1]
    cycle_size = lax.axis_size("modes")
    quarter = col_count // GROUPS
    own_index = lax.axis_index("modes")
    pix_index = lax.axis_index("pix")
    x, y, core = spot(own_index % HALF)

    pieces = [
        jnp.dot(pack, lax.dynamic_slice_in_dim(weighted_modes, (pix_index ^ k) * quarter, quarter, 1))
        for k in range(GROUPS)
    ]
    masked = jnp.dot(pack, pixel_modes)

    def in_order(got):
        out = jnp.zeros((GROUPS * row_count, quarter), jnp.bfloat16)
        for k in range(GROUPS):
            out = lax.dynamic_update_slice_in_dim(out, got[k], (pix_index ^ k) * row_count, 0)
        return out

    swapped = [move(pieces[k], pix_partner(k)) for k in range(1, GROUPS)]
    early = [move(pieces[k], across(k, 3)) for k in (0, 3)]
    late = move(jnp.concatenate([pieces[1], pieces[2]]), around)
    masked, swapped, early, late = lax.optimization_barrier((masked, swapped, early, late))

    full = lax.all_gather(masked, "pix", axis=0, tiled=True)
    carried = in_order([pieces[0]] + swapped)
    early = move(jnp.concatenate(early), around)
    late = [move(late[:row_count], across(1, 0)), move(late[row_count:], across(2, 0))]
    early, late = lax.optimization_barrier((early, late))
    crossed = in_order([early[:row_count]] + late + [early[row_count:]])
    previous = jnp.where(x == 0, crossed, move(carried, next_row))

    near = jnp.where(y < 1, move(previous, along_row(1, True)), move(carried, along_row(1, False)))
    far = jnp.where(y < 2, move(previous, along_row(2, True)), move(carried, along_row(2, False)))
    last = jnp.where(
        y < 3, move(previous, along_row(3, True, True)), move(carried, along_row(3, False, True))
    )
    first = move(jnp.where(core == 0, carried, near), other_core)
    third = move(jnp.where(core == 0, near, far), other_core)
    fifth = jnp.where(core == 0, last, move(far, core_up))
    partners = [first, near, third, far, fifth]

    own_bins = lax.dynamic_slice_in_dim(mode_bins, own_index * col_count, col_count, 0)
    partner_bins = []
    for turn_index in range(ROUNDS):
        owner_index = jnp.mod(own_index - turn_index - 1, cycle_size)
        partner_bins.append(
            lax.dynamic_slice_in_dim(
                mode_bins, owner_index * col_count + pix_index * quarter, quarter, 0
            )
        )
    binned = bin_tiles(full, partners, own_bins, jnp.stack(partner_bins))
    return sum_over_pix(binned, pix_index)[None]


def shards(pixel_modes, weighted_modes, mode_bins, live_counts):
    most = largest_over_pix(jnp.sum(live_counts))
    pack = packing(live_counts)
    level = sum((most > size).astype(jnp.int32) for size in SIZES[:-1])
    branches = [functools.partial(tiles, size) for size in SIZES]
    return lax.switch(level, branches, pack, pixel_modes, weighted_modes, mode_bins)


def solution(mesh):
    in_specs = (P("pix", "modes"), P("pix", "modes"), P(), P("pix", None))
    out_specs = P("modes", None, None, None)
    return jax.shard_map(shards, mesh=mesh, in_specs=in_specs, out_specs=out_specs, check_vma=False)
```

```python
import functools

import jax
import jax.numpy as jnp
from jax import lax
from jax.experimental import pallas as pl
from jax.experimental.pallas import tpu as pltpu
from jax.sharding import PartitionSpec as P

NB = 128
ROW_BLOCK = 128
ROUNDS = 5
GROUPS = 4
HALF = 32
CHUNKS = 3
SIZES = (512, 448, 320, 384)


def move(block, route):
    pairs = []
    for half in range(2):
        for place in range(HALF):
            for p in range(GROUPS):
                target = route(half, place, p)
                if target is not None:
                    source = (half * HALF + place) * GROUPS + p
                    pairs.append((source, (target[0] * HALF + target[1]) * GROUPS + target[2]))
    return lax.ppermute(block, ("modes", "pix"), pairs)


def spot(place):
    return place // 8, (place // 2) % 4, place % 2


def seat(x, y, core):
    return (x * 4 + y) * 2 + core


def trails(y, core):
    return 2 * y + core >= 8 - ROUNDS


def next_row(half, place, p):
    x, y, core = spot(place)
    return (half, seat(x + 1, y, core), p) if x < 3 and trails(y, core) else None


def across(k, column):
    def route(half, place, p):
        x, y, core = spot(place)
        return (1 - half, place, p ^ k) if x == column and trails(y, core) else None

    return route


def around(half, place, p):
    x, y, core = spot(place)
    return (half, seat(0, y, core), p) if x == 3 and trails(y, core) else None


def along_row(chips, rows, core=None):
    def route(half, place, p):
        x, y, own_core = spot(place)
        if y not in rows or core not in (None, own_core):
            return None
        return half, seat(x, (y + chips) % 4, own_core), p

    return route


def either(first, second):
    return lambda *device: first(*device) or second(*device)


def other_core(half, place, p):
    return half, place ^ 1, p


def pix_partner(k):
    return lambda half, place, p: (half, place, p ^ k)


def bin_kernel(place_ref, own_ref, partner_ref, full_ref, *rest):
    partner_cols, (out_ref, full, partner, own_table, full_sems, partner_sems) = rest[:ROUNDS], rest[ROUNDS:]
    quarter = partner.shape[2]
    width = full.shape[1] // CHUNKS

    rows = full.shape[0] // GROUPS

    def full_copy(c, k):
        part = pl.ds(c * width, width)
        source = pl.multiple_of((place_ref[0] ^ k) * rows, 16)
        return pltpu.make_async_copy(
            full_ref.at[pl.ds(source, rows), part],
            full.at[pl.ds(k * rows, rows), part],
            full_sems.at[c, k],
        )

    def partner_copy(source, r):
        return pltpu.make_async_copy(partner_cols[source], partner.at[r], partner_sems.at[r])

    core = place_ref[1]
    rounds = (4 - 4 * core, 1, 2 * core, 3, 2 + 2 * core)
    for source in (0, 2):
        partner_copy(source, rounds[source]).start()
    for c in range(CHUNKS):
        for k in range(GROUPS):
            full_copy(c, k).start()
    for source in (1, 4, 3):
        partner_copy(source, rounds[source]).start()
    bins = lax.broadcasted_iota(jnp.int32, (NB, 1), 0)
    own_table[...] = (bins == own_ref[...]).astype(jnp.bfloat16).T

    def parts(values):
        high = values.astype(jnp.bfloat16)
        return high, (values - high.astype(jnp.float32)).astype(jnp.bfloat16)

    def product(r, c):
        if c == 0:
            partner_copy(r, r).wait()
        if r == 0:
            for k in range(GROUPS):
                full_copy(c, k).wait()
        return lax.dot_general(
            partner[r], full[:, c * width : (c + 1) * width], (((0,), (0,)), ((), ())),
            preferred_element_type=jnp.float32,
        )

    steps = [(r, c) for r in range(ROUNDS) for c in range(CHUNKS)]
    upcoming = product(0, 0)
    for step, (r, c) in enumerate(steps):
        tile = upcoming
        if step + 1 < len(steps):
            upcoming = product(*steps[step + 1])
        if c == 0:
            left = jnp.zeros((quarter, NB), jnp.float32)
        for part in parts(tile * tile):
            left = left + jnp.dot(
                part, own_table[c * width : (c + 1) * width, :], preferred_element_type=jnp.float32
            )
        if c == CHUNKS - 1:
            table = (bins == partner_ref[r : r + 1, :]).astype(jnp.bfloat16)
            total = jnp.zeros((NB, NB), jnp.float32)
            for part in parts(left):
                total = total + jnp.dot(table, part, preferred_element_type=jnp.float32)
            out_ref[r] = (0.5 * total).T


def bin_tiles(pix_index, core, full, partners, own_bins, partner_bins):
    depth, col_count = full.shape
    quarter = partners[0].shape[1]
    whole = pl.BlockSpec(memory_space=pltpu.VMEM)
    anywhere = pl.BlockSpec(memory_space=pl.ANY)
    macs = ROUNDS * depth * col_count * quarter
    return pl.pallas_call(
        bin_kernel,
        out_shape=jax.ShapeDtypeStruct((ROUNDS, NB, NB), jnp.float32),
        in_specs=[pl.BlockSpec(memory_space=pltpu.SMEM), whole, whole] + [anywhere] * (1 + ROUNDS),
        out_specs=whole,
        scratch_shapes=[
            pltpu.VMEM((depth, col_count), jnp.bfloat16),
            pltpu.VMEM((ROUNDS, depth, quarter), jnp.bfloat16),
            pltpu.VMEM((col_count, NB), jnp.bfloat16),
            pltpu.SemaphoreType.DMA((CHUNKS, GROUPS)),
            pltpu.SemaphoreType.DMA((ROUNDS,)),
        ],
        compiler_params=pltpu.CompilerParams(vmem_limit_bytes=56 * 1024 * 1024),
        cost_estimate=pl.CostEstimate(
            flops=3 * macs, bytes_accessed=2 * depth * (col_count + ROUNDS * quarter), transcendentals=0
        ),
    )(jnp.stack([pix_index, core]), own_bins[None, :], partner_bins, full, *partners)


def sum_over_pix(part, pix_index):
    rows = NB // GROUPS

    def piece(k):
        return lax.dynamic_slice_in_dim(part, (pix_index ^ k) * rows, rows, 1)

    total = piece(0)
    for k in range(1, GROUPS):
        total = total + move(piece(k), pix_partner(k))
    out = jnp.zeros_like(part)
    for k in range(GROUPS):
        got = total if k == 0 else move(total, pix_partner(k))
        out = lax.dynamic_update_slice_in_dim(out, got, (pix_index ^ k) * rows, 1)
    return out


def packing(live_counts):
    counts = live_counts.reshape(-1)
    ends = jnp.cumsum(counts)
    offsets = jnp.arange(ROW_BLOCK, dtype=jnp.int32)[None, :]
    places = jnp.where(offsets < counts[:, None], (ends - counts)[:, None] + offsets, -1).reshape(-1)
    return (jnp.arange(places.shape[0], dtype=jnp.int32)[:, None] == places[None, :]).astype(jnp.bfloat16)


def largest_over_pix(count):
    held = jnp.full((8, 128), count, jnp.float32)
    most = held
    for k in range(1, GROUPS):
        most = jnp.maximum(most, move(held, pix_partner(k)))
    return most[0, 0].astype(jnp.int32)


def tiles(row_count, masked, pieces, mode_bins):
    masked = masked[:row_count]
    col_count = masked.shape[1]
    cycle_size = lax.axis_size("modes")
    quarter = col_count // GROUPS
    own_index = lax.axis_index("modes")
    pix_index = lax.axis_index("pix")
    x, y, core = spot(own_index % HALF)

    pieces = [piece[:row_count] for piece in pieces]
    swapped = [move(pieces[k], pix_partner(k)) for k in range(1, GROUPS)]
    early = [move(pieces[k], across(k, 3)) for k in (0, 3)]
    late = [move(pieces[k], around) for k in (1, 2)]
    swapped, early, late = lax.optimization_barrier((swapped, early, late))
    full = lax.all_gather(masked, "pix", axis=0, tiled=True)
    carried = jnp.concatenate([pieces[0]] + swapped)
    early = [move(piece, around) for piece in early]
    late = [move(piece, across(k, 0)) for k, piece in zip((1, 2), late)]
    early, late = lax.optimization_barrier((early, late))
    previous = move(carried, next_row)
    for k, crossed in enumerate([early[0]] + late + [early[1]]):
        moved = previous[k * row_count : (k + 1) * row_count]
        previous = lax.dynamic_update_slice_in_dim(
            previous, jnp.where(x == 0, crossed, moved), k * row_count, 0
        )

    near = jnp.where(
        y == 0, move(previous, along_row(1, (3,))), move(carried, along_row(1, (0, 1, 2)))
    )
    back = jnp.where(
        y == 3, move(carried, along_row(-1, (0,), 1)), move(previous, along_row(-1, (1, 2, 3), 1))
    )
    hop = move(
        jnp.where(core == 0, previous, carried), either(along_row(1, (2,), 0), along_row(-1, (1,), 1))
    )
    onward = jnp.where(y == 3 - 3 * core, hop, jnp.where(core == 0, near, back))
    every = (0, 1, 2, 3)
    far = move(onward, either(along_row(1, every, 0), along_row(-1, every, 1)))
    other_near = move(near, other_core)
    other_far = move(far, other_core)
    mixed = move(jnp.where(core == 0, carried, back), other_core)
    partners = [mixed, near, other_near, far, other_far]

    own_bins = lax.dynamic_slice_in_dim(mode_bins, own_index * col_count, col_count, 0)
    partner_bins = []
    for turn_index in range(ROUNDS):
        owner_index = jnp.mod(own_index - turn_index - 1, cycle_size)
        partner_bins.append(
            lax.dynamic_slice_in_dim(
                mode_bins, owner_index * col_count + pix_index * quarter, quarter, 0
            )
        )
    binned = bin_tiles(pix_index, core, full, partners, own_bins, jnp.stack(partner_bins))
    return sum_over_pix(binned, pix_index)[None]


def shards(pixel_modes, weighted_modes, mode_bins, live_counts):
    most = largest_over_pix(jnp.sum(live_counts))
    pack = packing(live_counts)
    masked = jnp.dot(pack, pixel_modes)
    weighted = jnp.dot(pack, weighted_modes)
    quarter = weighted.shape[1] // GROUPS
    pieces = [
        lax.dynamic_slice_in_dim(weighted, (lax.axis_index("pix") ^ k) * quarter, quarter, 1)
        for k in range(GROUPS)
    ]
    branch = SIZES.index(max(SIZES))
    for size in sorted(SIZES, reverse=True)[1:]:
        branch = jnp.where(most <= size, SIZES.index(size), branch)
    branches = [functools.partial(tiles, size) for size in SIZES]
    return lax.switch(branch, branches, masked, pieces, mode_bins)


def solution(mesh):
    in_specs = (P("pix", "modes"), P("pix", "modes"), P(), P("pix", None))
    out_specs = P("modes", None, None, None)
    return jax.shard_map(shards, mesh=mesh, in_specs=in_specs, out_specs=out_specs, check_vma=False)
```

```python
import functools

import jax
import jax.numpy as jnp
from jax import lax
from jax.experimental import pallas as pl
from jax.experimental.pallas import tpu as pltpu
from jax.sharding import PartitionSpec as P

NB = 128
ROW_BLOCK = 128
ROUNDS = 5
GROUPS = 4
HALF = 32
CHUNKS = 3
SIZES = (512, 448, 320, 384)


def move(block, route):
    pairs = []
    for half in range(2):
        for place in range(HALF):
            for p in range(GROUPS):
                target = route(half, place, p)
                if target is not None:
                    source = (half * HALF + place) * GROUPS + p
                    pairs.append((source, (target[0] * HALF + target[1]) * GROUPS + target[2]))
    return lax.ppermute(block, ("modes", "pix"), pairs)


def spot(place):
    return place // 8, (place // 2) % 4, place % 2


def seat(x, y, core):
    return (x * 4 + y) * 2 + core


def trails(y, core):
    return 2 * y + core >= 8 - ROUNDS


def next_row(half, place, p):
    x, y, core = spot(place)
    return (half, seat(x + 1, y, core), p) if x < 3 and trails(y, core) else None


def across(k, column):
    def route(half, place, p):
        x, y, core = spot(place)
        return (1 - half, place, p ^ k) if x == column and trails(y, core) else None

    return route


def around(half, place, p):
    x, y, core = spot(place)
    return (half, seat(0, y, core), p) if x == 3 and trails(y, core) else None


def along_row(chips, rows, core=None):
    def route(half, place, p):
        x, y, own_core = spot(place)
        if y not in rows or core not in (None, own_core):
            return None
        return half, seat(x, (y + chips) % 4, own_core), p

    return route


def along_line(step, places):
    return lambda half, place, p: (half, place, p + step) if p in places else None


def either(first, second):
    return lambda *device: first(*device) or second(*device)


def other_core(half, place, p):
    return half, place ^ 1, p


def pix_partner(k):
    return lambda half, place, p: (half, place, p ^ k)


def bin_kernel(place_ref, own_ref, partner_ref, *rest):
    lines, rest = rest[: 2 * GROUPS - 1], rest[2 * GROUPS - 1 :]
    partner_cols, (out_ref, full, partner, own_table, full_sems, partner_sems) = rest[:ROUNDS], rest[ROUNDS:]
    quarter = partner.shape[2]
    width = full.shape[1] // CHUNKS

    rows = full.shape[0] // GROUPS

    def full_copy(c, k, line=0):
        part = pl.ds(c * width, width)
        return pltpu.make_async_copy(
            lines[line].at[:, part], full.at[pl.ds(k * rows, rows), part], full_sems.at[c, k]
        )

    def start_full(p):
        for c in range(CHUNKS):
            for k in range(GROUPS):
                away = (p ^ k) - p
                full_copy(c, k, -away if away <= 0 else GROUPS - 1 + away).start()

    def partner_copy(source, r):
        return pltpu.make_async_copy(partner_cols[source], partner.at[r], partner_sems.at[r])

    core = place_ref[1]
    rounds = (4 - 4 * core, 1, 2 * core, 3, 2 + 2 * core)
    for source in (0, 2):
        partner_copy(source, rounds[source]).start()
    for p in range(GROUPS):
        pl.when(place_ref[0] == p)(functools.partial(start_full, p))
    for source in (1, 4, 3):
        partner_copy(source, rounds[source]).start()
    bins = lax.broadcasted_iota(jnp.int32, (NB, 1), 0)
    own_table[...] = (bins == own_ref[...]).astype(jnp.bfloat16).T

    def parts(values):
        high = values.astype(jnp.bfloat16)
        return high, (values - high.astype(jnp.float32)).astype(jnp.bfloat16)

    def product(r, c):
        if c == 0:
            partner_copy(r, r).wait()
        if r == 0:
            for k in range(GROUPS):
                full_copy(c, k).wait()
        return lax.dot_general(
            partner[r], full[:, c * width : (c + 1) * width], (((0,), (0,)), ((), ())),
            preferred_element_type=jnp.float32,
        )

    steps = [(r, c) for r in range(ROUNDS) for c in range(CHUNKS)]
    upcoming = product(0, 0)
    for step, (r, c) in enumerate(steps):
        tile = upcoming
        if step + 1 < len(steps):
            upcoming = product(*steps[step + 1])
        if c == 0:
            left = jnp.zeros((quarter, NB), jnp.float32)
        for part in parts(tile * tile):
            left = left + jnp.dot(
                part, own_table[c * width : (c + 1) * width, :], preferred_element_type=jnp.float32
            )
        if c == CHUNKS - 1:
            table = (bins == partner_ref[r : r + 1, :]).astype(jnp.bfloat16)
            total = jnp.zeros((NB, NB), jnp.float32)
            for part in parts(left):
                total = total + jnp.dot(table, part, preferred_element_type=jnp.float32)
            out_ref[r] = (0.5 * total).T


def bin_tiles(pix_index, core, full, partners, own_bins, partner_bins):
    depth, col_count = partners[0].shape[0], own_bins.shape[0]
    quarter = partners[0].shape[1]
    whole = pl.BlockSpec(memory_space=pltpu.VMEM)
    anywhere = pl.BlockSpec(memory_space=pl.ANY)
    macs = ROUNDS * depth * col_count * quarter
    return pl.pallas_call(
        bin_kernel,
        out_shape=jax.ShapeDtypeStruct((ROUNDS, NB, NB), jnp.float32),
        in_specs=[pl.BlockSpec(memory_space=pltpu.SMEM), whole, whole] + [anywhere] * (2 * GROUPS - 1 + ROUNDS),
        out_specs=whole,
        scratch_shapes=[
            pltpu.VMEM((depth, col_count), jnp.bfloat16),
            pltpu.VMEM((ROUNDS, depth, quarter), jnp.bfloat16),
            pltpu.VMEM((col_count, NB), jnp.bfloat16),
            pltpu.SemaphoreType.DMA((CHUNKS, GROUPS)),
            pltpu.SemaphoreType.DMA((ROUNDS,)),
        ],
        compiler_params=pltpu.CompilerParams(vmem_limit_bytes=56 * 1024 * 1024),
        cost_estimate=pl.CostEstimate(
            flops=3 * macs, bytes_accessed=2 * depth * (col_count + ROUNDS * quarter), transcendentals=0
        ),
    )(jnp.stack([pix_index, core]), own_bins[None, :], partner_bins, *full, *partners)


def sum_over_pix(part, pix_index):
    rows = NB // GROUPS

    def piece(k):
        return lax.dynamic_slice_in_dim(part, (pix_index ^ k) * rows, rows, 1)

    total = piece(0)
    for k in range(1, GROUPS):
        total = total + move(piece(k), pix_partner(k))
    out = jnp.zeros_like(part)
    for k in range(GROUPS):
        got = total if k == 0 else move(total, pix_partner(k))
        out = lax.dynamic_update_slice_in_dim(out, got, (pix_index ^ k) * rows, 1)
    return out


def packing(live_counts):
    counts = live_counts.reshape(-1)
    ends = jnp.cumsum(counts)
    offsets = jnp.arange(ROW_BLOCK, dtype=jnp.int32)[None, :]
    places = jnp.where(offsets < counts[:, None], (ends - counts)[:, None] + offsets, -1).reshape(-1)
    return (jnp.arange(places.shape[0], dtype=jnp.int32)[:, None] == places[None, :]).astype(jnp.bfloat16)


def largest_over_pix(count):
    held = jnp.full((8, 128), count, jnp.float32)
    most = held
    for k in range(1, GROUPS):
        most = jnp.maximum(most, move(held, pix_partner(k)))
    return most[0, 0].astype(jnp.int32)


def tiles(row_count, masked, weighted, mode_bins):
    masked = masked[:row_count]
    col_count = masked.shape[1]
    cycle_size = lax.axis_size("modes")
    quarter = col_count // GROUPS
    own_index = lax.axis_index("modes")
    pix_index = lax.axis_index("pix")
    x, y, core = spot(own_index % HALF)

    pieces = [
        lax.dynamic_slice(weighted, (0, (pix_index ^ k) * quarter), (row_count, quarter))
        for k in range(GROUPS)
    ]
    swapped = [move(pieces[k], pix_partner(k)) for k in range(1, GROUPS)]
    early = [move(pieces[k], across(k, 3)) for k in (0, 3)]
    late = [move(pieces[k], around) for k in (1, 2)]
    swapped, early, late = lax.optimization_barrier((swapped, early, late))
    carried = jnp.concatenate([pieces[0]] + swapped)
    early = [move(piece, around) for piece in early]
    late = [move(piece, across(k, 0)) for k, piece in zip((1, 2), late)]
    early, late = lax.optimization_barrier((early, late))
    previous = move(carried, next_row)
    for k, crossed in enumerate([early[0]] + late + [early[1]]):
        moved = previous[k * row_count : (k + 1) * row_count]
        previous = lax.dynamic_update_slice_in_dim(
            previous, jnp.where(x == 0, crossed, moved), k * row_count, 0
        )

    near = jnp.where(
        y == 0, move(previous, along_row(1, (3,))), move(carried, along_row(1, (0, 1, 2)))
    )
    back = jnp.where(
        y == 3, move(carried, along_row(-1, (0,), 1)), move(previous, along_row(-1, (1, 2, 3), 1))
    )
    hop = move(
        jnp.where(core == 0, previous, carried), either(along_row(1, (2,), 0), along_row(-1, (1,), 1))
    )
    onward = jnp.where(y == 3 - 3 * core, hop, jnp.where(core == 0, near, back))
    every = (0, 1, 2, 3)
    far = move(onward, either(along_row(1, every, 0), along_row(-1, every, 1)))
    other_near = move(near, other_core)
    other_far = move(far, other_core)
    mixed = move(jnp.where(core == 0, carried, back), other_core)
    partners = [mixed, near, other_near, far, other_far]

    ups, downs = [masked], [masked]
    for steps in range(1, GROUPS):
        ups.append(move(ups[-1], along_line(1, range(steps - 1, GROUPS - 1))))
        downs.append(move(downs[-1], along_line(-1, range(1, GROUPS - steps + 1))))
    full = ups + downs[1:]

    own_bins = lax.dynamic_slice_in_dim(mode_bins, own_index * col_count, col_count, 0)
    partner_bins = []
    for turn_index in range(ROUNDS):
        owner_index = jnp.mod(own_index - turn_index - 1, cycle_size)
        partner_bins.append(
            lax.dynamic_slice_in_dim(
                mode_bins, owner_index * col_count + pix_index * quarter, quarter, 0
            )
        )
    binned = bin_tiles(pix_index, core, full, partners, own_bins, jnp.stack(partner_bins))
    return sum_over_pix(binned, pix_index)[None]


def shards(pixel_modes, weighted_modes, mode_bins, live_counts):
    most = largest_over_pix(jnp.sum(live_counts))
    pack = packing(live_counts)
    masked = jnp.dot(pack, pixel_modes)
    weighted = jnp.dot(pack, weighted_modes)
    branch = SIZES.index(max(SIZES))
    for size in sorted(SIZES, reverse=True)[1:]:
        branch = jnp.where(most <= size, SIZES.index(size), branch)
    branches = [functools.partial(tiles, size) for size in SIZES]
    return lax.switch(branch, branches, masked, weighted, mode_bins)


def solution(mesh):
    in_specs = (P("pix", "modes"), P("pix", "modes"), P(), P("pix", None))
    out_specs = P("modes", None, None, None)
    return jax.shard_map(shards, mesh=mesh, in_specs=in_specs, out_specs=out_specs, check_vma=False)
```
